128 devices in a mesh: head: 4 (over y_lo, core), inner: 8 (over y_hi, x), outer: 4 (over z).
Axes of the slice: x: 4, y: 4 (y_hi: 2, y_lo: 2; y = y_hi * 2 + y_lo), z: 4, core: 2. Of those that a mesh axis runs over, the one named last changes fastest.
Arguments:
- queries: bfloat16 [8192, 4096], P(('head', 'inner', 'outer')), may hold values from -11 to 11
- keys: bfloat16 [8192, 512], P(('head', 'inner', 'outer')), may hold values from -11 to 11
- values: bfloat16 [8192, 512], P(('head', 'inner', 'outer')), may hold values from -6 to 6
- outputs: bfloat16 [8192, 4096], P(('head', 'inner', 'outer')), may hold values from -6 to 6
- out_grads: bfloat16 [8192, 4096], P(('head', 'inner', 'outer')), may hold values from -6 to 6
- block_order: int32 [128], replicated, may hold values from 0 to 127, each once
- segment_ids: int32 [8192], replicated, may hold values from 0 to 3, never falling along the last dimension, each value on 1 to 4096 neighbouring positions
Outputs:
- grad_queries: bfloat16 [8192, 4096], P(('head', 'inner', 'outer'))
- grad_keys: bfloat16 [8192, 512], P(('head', 'inner', 'outer'))
- grad_values: bfloat16 [8192, 512], P(('head', 'inner', 'outer'))
The draws below stay inside these ranges and needn't reach their ends.
Inputs may be any that keep to these rules, and one draw needn't show every extreme that they name: `block_order`: a permutation of the 128 position blocks. `segment_ids`: document numbers never fall along positions; each document has 1 to 4096 positions, one exactly 4096.
All inputs are finite; a program needn't handle non-finite values.
Results may differ from the reference program's by a relative error of at most 0.0049.
Values may be sent and summed in bfloat16 or wider, within the bound.
No kernel may reach another device: no remote copies, remote signals or barrier semaphores. Data moves between devices by JAX's collectives and lax.ppermute only.
A program may use at most 64 MiB of HBM per device.

```python
import math
import jax
import jax.numpy as jnp
import numpy as np
from jax import lax

HQ = 32
KVH = 4
DH = 128
DOCS = 4
SEQ = 8192
BLOCKS = 128
DOC_MOST = 4096


def draw_queries(key, part):
    key = jax.random.fold_in(key, 1)
    first = jax.random.fold_in(key, 0)
    result = jnp.clip(jax.random.normal(first, (SEQ, HQ, DH), jnp.float32), -4.0, 4.0)
    return result.reshape(SEQ, HQ * DH).astype(jnp.bfloat16)


def draw_keys(key, part):
    key = jax.random.fold_in(key, 2)
    first = jax.random.fold_in(key, 0)
    result = jnp.clip(jax.random.normal(first, (SEQ, KVH, DH), jnp.float32), -4.0, 4.0)
    return result.reshape(SEQ, KVH * DH).astype(jnp.bfloat16)


def shard_levels(key, dims, shards, least, largest):
    factor_of = 1.0
    for dim, blocks in shards:
        draws = jax.random.uniform(jax.random.fold_in(jax.random.fold_in(key, 6), dim), (blocks,), jnp.float32, least / len(shards), largest / len(shards))
        factor_of = factor_of * jnp.repeat(jnp.exp(draws), dims[dim] // blocks).reshape((-1,) + (1,) * (len(dims) - 1 - dim))
    return factor_of


def profile(count, total, bound, skew):
    portions = [(1 << 20) // math.isqrt(standing ** skew) + 1 for standing in range(2, count + 1)]
    rest, given = total - bound - (count - 1), [1] * (count - 1)
    while rest > 0:
        free = [i for i in range(count - 1) if given[i] < bound]
        whole, remaining = sum([portions[i] for i in free]), rest
        for i in free:
            addition = min(bound - given[i], max(1, remaining * portions[i] // whole), rest)
            given[i] = given[i] + addition
            rest = rest - addition
    return np.array([bound] + given)


def uneven(key, amount, total, bound, skew):
    if amount == 2:
        one = jax.random.randint(key, (), max(1, total - bound), min(bound, total - 1) + 1)
        return jnp.stack([one, total - one])
    tallies = jnp.asarray(profile(amount, total, bound, skew), jnp.int32)
    couples = (amount - 1) // 2
    donor, sink = tallies[1:1 + 2 * couples:2], tallies[2:2 + 2 * couples:2]
    margin = jnp.minimum(donor - 1, bound - sink)
    moved = jax.random.randint(jax.random.fold_in(key, 1), (couples,), 0, 1 << 20) % (margin + 1)
    tallies = tallies.at[1:1 + 2 * couples:2].set(donor - moved).at[2:2 + 2 * couples:2].set(sink + moved)
    return tallies[jax.random.permutation(jax.random.fold_in(key, 2), amount)]


def scatter_about(stream_key, shape, scale, most, cuts=(), kind=jnp.bfloat16):
    drawn = scale * jax.random.normal(stream_key, shape, jnp.float32)
    if cuts:
        drawn = drawn * shard_levels(stream_key, shape, cuts, -0.22, 0.18)
    return jnp.clip(drawn, -most, most).astype(kind)


def setup_inputs(seed: int = 0) -> dict:
    streams_of = jax.random.split(jax.random.key(seed), 8)
    queries = draw_queries(jax.random.fold_in(streams_of[7], 71), 0)
    keys = draw_keys(jax.random.fold_in(streams_of[7], 71), 0)
    values = scatter_about(streams_of[2], (SEQ, KVH * DH), 1.0, 6.0, ((0, 128),))
    outputs = scatter_about(streams_of[3], (SEQ, HQ * DH), 1.0, 6.0, ((0, 128),))
    out_grads = scatter_about(streams_of[4], (SEQ, HQ * DH), 1.0, 6.0, ((0, 128),))
    block_order = jax.random.permutation(streams_of[5], BLOCKS).astype(jnp.int32)
    segment_ids = jnp.searchsorted(jnp.cumsum(uneven(streams_of[6], DOCS, SEQ, DOC_MOST, 0)), jnp.arange(SEQ), side="right").astype(jnp.int32)
    return dict(queries=queries, keys=keys, values=values, outputs=outputs, out_grads=out_grads, block_order=block_order, segment_ids=segment_ids)


big_negative = -1e+30

def rounded(value):
    return lax.optimization_barrier(value.astype(jnp.bfloat16)).astype(jnp.float32)

def reference(queries, keys, values, outputs, out_grads, block_order, segment_ids):
    rows = jnp.arange(SEQ, dtype=jnp.int32)
    width = SEQ // BLOCKS
    positions = (jnp.take(block_order, rows // width) * width + rows % width).astype(jnp.int32)
    docs = jnp.take(segment_ids, positions).astype(jnp.int32)
    group = HQ // KVH
    scale = 1.0 / math.sqrt(DH)
    query_heads = queries.reshape(SEQ, KVH, group, DH).transpose(1, 0, 2, 3)
    grad_heads = out_grads.reshape(SEQ, KVH, group, DH).transpose(1, 0, 2, 3)
    key_heads = keys.reshape(SEQ, KVH, DH).transpose(1, 0, 2)
    value_heads = values.reshape(SEQ, KVH, DH).transpose(1, 0, 2)
    products = out_grads.astype(jnp.float32) * outputs.astype(jnp.float32)
    delta = lax.optimization_barrier(jnp.sum(products.reshape(SEQ, KVH, group, DH), axis=-1)).transpose(1, 2, 0)
    block_rows = math.gcd(SEQ, 512)

    def one_group(items):
        query_group, grad_group, key_group, value_group, delta_group = items
        key_float = key_group.astype(jnp.float32)
        value_float = value_group.astype(jnp.float32)

        def step(carry, index):
            grad_k, grad_v = carry
            begin = (index * block_rows).astype(jnp.int32)
            query_block = lax.dynamic_slice_in_dim(query_group, begin, block_rows, 0).astype(jnp.float32)
            grad_block = lax.dynamic_slice_in_dim(grad_group, begin, block_rows, 0).astype(jnp.float32)
            delta_block = lax.dynamic_slice_in_dim(delta_group, begin, block_rows, 1)
            query_pos = lax.dynamic_slice_in_dim(positions, begin, block_rows, 0)
            query_doc = lax.dynamic_slice_in_dim(docs, begin, block_rows, 0)
            allowed = (positions[None, :] <= query_pos[:, None]) & (docs[None, :] == query_doc[:, None])
            scores = jnp.einsum('trd,nd->rtn', query_block, key_float) * scale
            scores = jnp.where(allowed[None], scores, big_negative)
            top = lax.optimization_barrier(jnp.max(scores, axis=-1, keepdims=True))
            total = lax.optimization_barrier(jnp.sum(jnp.where(allowed[None], jnp.exp(scores - top), 0.0), axis=-1, keepdims=True))
            lse = top + jnp.log(total)
            prob = jnp.where(allowed[None], jnp.exp(scores - lse), 0.0)
            prob_b = rounded(prob)
            dprob = jnp.einsum('trd,nd->rtn', grad_block, value_float)
            dscore = rounded(prob * (dprob - delta_block[:, :, None]) * scale)
            grad_v = grad_v + jnp.einsum('rtn,trd->nd', prob_b, grad_block)
            grad_k = grad_k + jnp.einsum('rtn,trd->nd', dscore, query_block)
            grad_q = jnp.einsum('rtn,nd->trd', dscore, key_float).astype(jnp.bfloat16)
            return ((grad_k, grad_v), grad_q)
        zeros = jnp.zeros((SEQ, DH), jnp.float32)
        (grad_k, grad_v), grad_q = lax.scan(step, (zeros, zeros), jnp.arange(SEQ // block_rows, dtype=jnp.int32))
        return (grad_q.reshape(SEQ, group, DH), grad_k.astype(jnp.bfloat16), grad_v.astype(jnp.bfloat16))
    grad_q, grad_k, grad_v = lax.map(one_group, (query_heads, grad_heads, key_heads, value_heads, delta))
    grad_queries = grad_q.transpose(1, 0, 2, 3).reshape(SEQ, HQ * DH)
    grad_keys = grad_k.transpose(1, 0, 2).reshape(SEQ, KVH * DH)
    grad_values = grad_v.transpose(1, 0, 2).reshape(SEQ, KVH * DH)
    return (grad_queries, grad_keys, grad_values)
```

```python
import math

import jax
import jax.numpy as jnp
from jax import lax
from jax.experimental import pallas as pl
from jax.experimental.pallas import tpu as pltpu
from jax.sharding import Mesh, PartitionSpec as P

HQ = 32
KVH = 4
DH = 128
ROWS = 64
SEQ = 8192
BLOCKS = 128
DOCS = 4
DOC_MOST = 4096
SLOTS = 8
HEADS = 4
LANES = HEADS * ROWS
TILE = 512
TILES = (DOC_MOST + ROWS) // TILE + 2
RUN = 16
PIECE = RUN * ROWS

SCALE = 1.0 / math.sqrt(DH)
LOG2E = 1.0 / math.log(2.0)

AXES = ("yl", "c", "yh", "x", "z")
SIZES = (2, 2, 2, 4, 4)
YC = ("yh", "yl", "c")
YX = ("yh", "yl", "x")
YZ = ("yh", "yl", "z")


def stored_block(yl, c, yh, x, z):
    return (((yl * 2 + c) * 2 + yh) * 4 + x) * 4 + z


def block_rows(index):
    return pl.ds(pl.multiple_of(index * ROWS, ROWS), ROWS)


def attend_kernel(*refs):
    order_ref, seg_ref, qg_ref, delta_ref = refs[:4]
    key_pieces, value_pieces = refs[4:12], refs[12:20]
    dq_ref, dk_mine, dk_other, dv_mine, dv_other = refs[20:25]
    k_ref, v_ref, dk_acc, dv_acc, e_ref, qt_ref, gt_ref, q_ref, g_ref, dqt_ref = refs[25:]
    c, x, z = lax.axis_index("c"), lax.axis_index("x"), lax.axis_index("z")

    def load(i, _):
        yh, yl, w = i // 8, (i // 4) % 2, i % 4
        src = block_rows(i)
        for core in range(2):
            sc = c if core == 0 else 1 - c
            for n in range(4):
                place = order_ref[stored_block(yl, sc, yh, w, (z + 4 - n) % 4)]
                k_ref[block_rows(place), :] = key_pieces[core * 4 + n][src, :]
                place = order_ref[stored_block(yl, sc, yh, (x + 4 - n) % 4, w)]
                v_ref[block_rows(place), :] = value_pieces[core * 4 + n][src, :]
        return 0

    lax.fori_loop(0, RUN, load, 0)

    dk_acc[...] = jnp.zeros_like(dk_acc)
    dv_acc[...] = jnp.zeros_like(dv_acc)
    seg = seg_ref[...]
    starts = [jnp.sum((seg < d).astype(jnp.int32)) for d in range(1, DOCS)]

    lane = lax.broadcasted_iota(jnp.int32, (1, LANES), 1)
    row_in_block = lane % ROWS
    tile_row = lax.broadcasted_iota(jnp.int32, (TILE, LANES), 0)

    def one_slot(s, _):
        place = order_ref[stored_block((s // 2) % 2, s % 2, s // 4, x, z)]
        first = place * ROWS
        lo = jnp.int32(0)
        lo_last = jnp.int32(0)
        row_pos = first + row_in_block
        row_lo = jnp.zeros((1, LANES), jnp.int32)
        for start in starts:
            lo = jnp.where(start <= first, start, lo)
            lo_last = jnp.where(start <= first + ROWS - 1, start, lo_last)
            row_lo = jnp.where(start <= row_pos, start, row_lo)
        t0 = lo // TILE
        t1 = (first + ROWS + TILE - 1) // TILE
        inner_lo = jnp.minimum((lo_last + TILE - 1) // TILE, t1)
        inner_hi = jnp.maximum(first // TILE, inner_lo)
        for h in range(HEADS):
            q_ref[h * ROWS:(h + 1) * ROWS, :] = qg_ref[s, :, h * DH:(h + 1) * DH]
            g_ref[h * ROWS:(h + 1) * ROWS, :] = qg_ref[s, :, (HEADS + h) * DH:(HEADS + h + 1) * DH]
        qt_ref[...] = q_ref[...].T
        gt_ref[...] = g_ref[...].T

        def scores(masked):
            def step(t, top):
                begin = pl.multiple_of(t * TILE, TILE)
                st = jnp.dot(
                    k_ref[pl.ds(begin, TILE), :], qt_ref[...], preferred_element_type=jnp.float32
                ) * (SCALE * LOG2E)
                if masked:
                    pos = tile_row + begin
                    st = jnp.where((pos <= row_pos) & (pos >= row_lo), st, -2e30)
                e_ref[pl.ds(pl.multiple_of((t - t0) * TILE, TILE), TILE), :] = st
                return jnp.maximum(top, jnp.max(st.reshape(TILE // 8, 8, LANES), axis=0))
            return step

        top = jnp.full((8, LANES), -1e30, jnp.float32)
        top = lax.fori_loop(t0, inner_lo, scores(True), top)
        top = lax.fori_loop(inner_lo, inner_hi, scores(False), top)
        top = lax.fori_loop(inner_hi, t1, scores(True), top)
        top = jnp.max(top, axis=0, keepdims=True)

        def exps(t, total):
            at = pl.ds(pl.multiple_of((t - t0) * TILE, TILE), TILE)
            e = jnp.exp2(e_ref[at, :] - top)
            e_ref[at, :] = e
            return total + jnp.sum(e.reshape(TILE // 8, 8, LANES), axis=0)

        total = lax.fori_loop(t0, t1, exps, jnp.zeros((8, LANES), jnp.float32))
        inverse = 1.0 / jnp.sum(total, axis=0, keepdims=True)
        delta = delta_ref[pl.ds(s, 1), :]
        dqt_ref[...] = jnp.zeros_like(dqt_ref)

        def grads(t, _):
            begin = pl.multiple_of(t * TILE, TILE)
            p = e_ref[pl.ds(pl.multiple_of((t - t0) * TILE, TILE), TILE), :] * inverse
            dp = jnp.dot(
                v_ref[pl.ds(begin, TILE), :], gt_ref[...], preferred_element_type=jnp.float32
            )
            pb = p.astype(jnp.bfloat16)
            ds = (p * (dp - delta) * SCALE).astype(jnp.bfloat16)
            dv_acc[pl.ds(begin, TILE), :] += jnp.dot(pb, g_ref[...], preferred_element_type=jnp.float32)
            dk_acc[pl.ds(begin, TILE), :] += jnp.dot(ds, q_ref[...], preferred_element_type=jnp.float32)
            dqt_ref[...] += lax.dot_general(
                k_ref[pl.ds(begin, TILE), :], ds, (((0,), (0,)), ((), ())),
                preferred_element_type=jnp.float32,
            )
            return 0

        lax.fori_loop(t0, t1, grads, 0)
        dq = dqt_ref[...].T.astype(jnp.bfloat16)
        for h in range(HEADS):
            dq_ref[s, :, h * DH:(h + 1) * DH] = dq[h * ROWS:(h + 1) * ROWS, :]
        return 0

    lax.fori_loop(0, SLOTS, one_slot, 0)

    def store(i, _):
        yh, yl, w = i // 8, (i // 4) % 2, i % 4
        for n in range(4):
            dst = block_rows(i + n * RUN)
            far_z, far_x = (z + n) % 4, (x + n) % 4
            for core in range(2):
                sc = c if core == 0 else 1 - c
                dk_out, dv_out = (dk_mine, dv_mine) if core == 0 else (dk_other, dv_other)
                place = order_ref[stored_block(yl, sc, yh, far_x, w)]
                dk_out[dst, :] = dk_acc[block_rows(place), :].astype(dk_out.dtype)
                place = order_ref[stored_block(yl, sc, yh, w, far_z)]
                dv_out[dst, :] = dv_acc[block_rows(place), :].astype(dv_out.dtype)
        return 0

    lax.fori_loop(0, RUN, store, 0)


def attend(order, seg, qg, delta, key_pieces, value_pieces):
    vmem = pl.BlockSpec(memory_space=pltpu.VMEM)
    half = (SEQ // 2, DH)
    return pl.pallas_call(
        attend_kernel,
        out_shape=(
            jax.ShapeDtypeStruct((SLOTS, ROWS, HEADS * DH), jnp.bfloat16),
            jax.ShapeDtypeStruct(half, jnp.float32),
            jax.ShapeDtypeStruct(half, jnp.bfloat16),
            jax.ShapeDtypeStruct(half, jnp.float32),
            jax.ShapeDtypeStruct(half, jnp.bfloat16),
        ),
        in_specs=[pl.BlockSpec(memory_space=pltpu.SMEM)] + [vmem] * 19,
        out_specs=(vmem,) * 5,
        scratch_shapes=[
            pltpu.VMEM((SEQ, DH), jnp.bfloat16),
            pltpu.VMEM((SEQ, DH), jnp.bfloat16),
            pltpu.VMEM((SEQ, DH), jnp.float32),
            pltpu.VMEM((SEQ, DH), jnp.float32),
            pltpu.VMEM((TILES * TILE, LANES), jnp.float32),
            pltpu.VMEM((DH, LANES), jnp.bfloat16),
            pltpu.VMEM((DH, LANES), jnp.bfloat16),
            pltpu.VMEM((LANES, DH), jnp.bfloat16),
            pltpu.VMEM((LANES, DH), jnp.bfloat16),
            pltpu.VMEM((DH, LANES), jnp.float32),
        ],
        compiler_params=pltpu.CompilerParams(vmem_limit_bytes=48 * 1024 * 1024),
        cost_estimate=pl.CostEstimate(
            flops=8 * 10**9, bytes_accessed=12 * 10**6, transcendentals=8 * 10**6
        ),
        name="attend",
    )(order, seg, qg, delta, *key_pieces, *value_pieces)


def exchange(value, axes):
    return lax.all_to_all(value, axes, split_axis=0, concat_axis=0, tiled=True)


def ahead(value, axis, n):
    return lax.ppermute(value, axis, [(i, (i + n) % 4) for i in range(4)])


def other_core(value):
    return lax.ppermute(value, "c", [(0, 1), (1, 0)])


def gathered(rows, axes, axis):
    groups = rows.reshape(ROWS, KVH, DH).transpose(1, 0, 2)
    copies = jnp.broadcast_to(groups[:, None], (KVH, 4, ROWS, DH)).reshape(RUN * ROWS, DH)
    own = exchange(copies, axes)
    pieces = [own] + [ahead(own, axis, n) for n in (1, 2, 3)]
    return pieces


def summed(mine, came, axes, axis):
    both = (mine + came.astype(jnp.float32)).astype(jnp.bfloat16).reshape(4, PIECE, DH)
    terms = [both[0]] + [ahead(both[n], axis, n) for n in (1, 2, 3)]
    part = sum(term.astype(jnp.float32) for term in terms).astype(jnp.bfloat16)
    parts = exchange(part, axes).reshape(KVH, 4, ROWS, DH)
    sums = jnp.sum(parts.astype(jnp.float32), axis=1).astype(jnp.bfloat16)
    return sums.transpose(1, 0, 2).reshape(ROWS, KVH * DH)


def per_device(queries, keys, values, outputs, out_grads, block_order, segment_ids):
    key_pieces = gathered(keys, YX, "z")
    value_pieces = gathered(values, YZ, "x")
    key_pieces += [other_core(piece) for piece in key_pieces]
    value_pieces += [other_core(piece) for piece in value_pieces]

    qg = jnp.concatenate(
        [queries.reshape(ROWS, SLOTS, HEADS * DH), out_grads.reshape(ROWS, SLOTS, HEADS * DH)],
        axis=-1,
    ).transpose(1, 0, 2)
    qg = exchange(qg, YC)
    products = outputs.astype(jnp.float32) * out_grads.astype(jnp.float32)
    delta = jnp.sum(products.reshape(ROWS, HQ, DH), axis=-1).T.reshape(SLOTS, LANES)
    delta = exchange(delta, YC)

    dq, dk_mine, dk_other, dv_mine, dv_other = attend(
        block_order, segment_ids.reshape(SEQ // 128, 128), qg, delta, key_pieces, value_pieces
    )
    dk_came, dv_came = other_core(dk_other), other_core(dv_other)
    grad_keys = summed(dk_mine, dk_came, YZ, "x")
    grad_values = summed(dv_mine, dv_came, YX, "z")
    grad_queries = exchange(dq, YC).transpose(1, 0, 2).reshape(ROWS, HQ * DH)
    return grad_queries, grad_keys, grad_values


def solution(mesh):
    split = Mesh(mesh.devices.reshape(SIZES), AXES)
    rows = P(AXES, None)
    return jax.shard_map(
        per_device,
        mesh=split,
        in_specs=(rows, rows, rows, rows, rows, P(), P()),
        out_specs=(rows, rows, rows),
        check_vma=False,
    )
```

```python
import math

import jax
import jax.numpy as jnp
from jax import lax
from jax.experimental import pallas as pl
from jax.experimental.pallas import tpu as pltpu
from jax.sharding import Mesh, PartitionSpec as P

HQ = 32
KVH = 4
DH = 128
ROWS = 64
SEQ = 8192
BLOCKS = 128
DOCS = 4
DOC_MOST = 4096
SLOTS = 8
HEADS = 4
LANES = HEADS * ROWS
TILE = 1024
TILES = (DOC_MOST + ROWS) // TILE + 2
RUN = 8
PIECE = RUN * ROWS

SCALE = 1.0 / math.sqrt(DH)
LOG2E = 1.0 / math.log(2.0)

AXES = ("yl", "c", "yh", "x", "z")
SIZES = (2, 2, 2, 4, 4)
YC = ("yh", "yl", "c")
Y = ("yh", "yl")


def stored_block(yl, c, yh, x, z):
    return (((yl * 2 + c) * 2 + yh) * 4 + x) * 4 + z


def block_rows(index):
    return pl.ds(pl.multiple_of(index * ROWS, ROWS), ROWS)


def attend_kernel(*refs):
    order_ref, seg_ref, qg_ref = refs[:3]
    pieces = refs[3:19]
    dq_ref, mine, other = refs[19], refs[20:28], refs[28:36]
    kv_ref, dk_acc, dv_acc, e_ref, qt_ref, gt_ref, q_ref, g_ref, dqt_ref, sem = refs[36:]
    c, x, z = lax.axis_index("c"), lax.axis_index("x"), lax.axis_index("z")

    def place_of(core, yh, far, i):
        near, yl = i // 2, i % 2
        sx, sz = (far, near) if yh == 0 else (near, far)
        sc = c if core == 0 else 1 - c
        return sc, yl, sx, sz

    def load(i, _):
        for core in range(2):
            for yh in range(2):
                for n in range(4):
                    sc, yl, sx, sz = place_of(core, yh, n, i)
                    place = order_ref[stored_block(yl, sc, yh, (x + 4 - sx) % 4, (z + 4 - sz) % 4)]
                    pltpu.make_async_copy(
                        pieces[(core * 2 + yh) * 4 + n].at[block_rows(i)],
                        kv_ref.at[block_rows(place)],
                        sem,
                    ).start()
        return 0

    lax.fori_loop(0, RUN, load, 0)

    kv_ref[SEQ:, :] = jnp.zeros((TILE, 2 * DH), jnp.bfloat16)
    dk_acc[...] = jnp.zeros_like(dk_acc)
    dv_acc[...] = jnp.zeros_like(dv_acc)
    seg = seg_ref[...]
    starts = [jnp.sum((seg < d).astype(jnp.int32)) for d in range(1, DOCS)]

    lane = lax.broadcasted_iota(jnp.int32, (1, LANES), 1)
    row_in_block = lane % ROWS
    tile_row = lax.broadcasted_iota(jnp.int32, (TILE, LANES), 0)
    whole = kv_ref.at[pl.ds(0, SEQ)]
    pltpu.make_async_copy(whole, whole, sem).wait()

    def one_slot(s, _):
        place = order_ref[stored_block((s // 2) % 2, s % 2, s // 4, x, z)]
        first = place * ROWS
        lo = jnp.int32(0)
        lo_last = jnp.int32(0)
        row_pos = first + row_in_block
        row_lo = jnp.zeros((1, LANES), jnp.int32)
        for start in starts:
            lo = jnp.where(start <= first, start, lo)
            lo_last = jnp.where(start <= first + ROWS - 1, start, lo_last)
            row_lo = jnp.where(start <= row_pos, start, row_lo)
        base = lo // ROWS * ROWS
        count = (first + ROWS - base + TILE - 1) // TILE
        inner_lo = jnp.minimum((lo_last - base + TILE - 1) // TILE, count)
        inner_hi = jnp.maximum((first - base) // TILE, inner_lo)
        for h in range(HEADS):
            q_ref[h * ROWS:(h + 1) * ROWS, :] = qg_ref[s, :, h * DH:(h + 1) * DH]
            g_ref[h * ROWS:(h + 1) * ROWS, :] = qg_ref[s, :, (HEADS + h) * DH:(HEADS + h + 1) * DH]
        qt_ref[...] = q_ref[...].T
        gt_ref[...] = g_ref[...].T
        parts = qg_ref[s, :16, 2 * HEADS * DH:].astype(jnp.float32)
        delta = jnp.concatenate(
            [parts[i:i + 1] + parts[i + 2:i + 3] + parts[i + 4:i + 5] for i in range(2)], axis=1
        )

        def rows_of(t):
            return pl.ds(pl.multiple_of(base + t * TILE, ROWS), TILE)

        def kept(t):
            return pl.ds(pl.multiple_of(t * TILE, TILE), TILE)

        def scores(masked):
            def step(t, top):
                st = jnp.dot(
                    kv_ref[rows_of(t), :DH], qt_ref[...], preferred_element_type=jnp.float32
                ) * (SCALE * LOG2E)
                if masked:
                    pos = tile_row + (base + t * TILE)
                    st = jnp.where((pos <= row_pos) & (pos >= row_lo), st, -2e30)
                e_ref[kept(t), :] = st
                return jnp.maximum(top, jnp.max(st.reshape(TILE // 8, 8, LANES), axis=0))
            return step

        top = jnp.full((8, LANES), -1e30, jnp.float32)
        top = lax.fori_loop(0, inner_lo, scores(True), top)
        top = lax.fori_loop(inner_lo, inner_hi, scores(False), top)
        top = lax.fori_loop(inner_hi, count, scores(True), top)
        top = jnp.max(top, axis=0, keepdims=True)

        def exps(t, total):
            e = jnp.exp2(e_ref[kept(t), :] - top)
            e_ref[kept(t), :] = e
            return total + jnp.sum(e.reshape(TILE // 8, 8, LANES), axis=0)

        total = lax.fori_loop(0, count, exps, jnp.zeros((8, LANES), jnp.float32))
        inverse = 1.0 / jnp.sum(total, axis=0, keepdims=True)
        dqt_ref[...] = jnp.zeros_like(dqt_ref)

        def grads(t, _):
            p = e_ref[kept(t), :] * inverse
            dp = jnp.dot(kv_ref[rows_of(t), DH:], gt_ref[...], preferred_element_type=jnp.float32)
            pb = p.astype(jnp.bfloat16)
            ds = (p * (dp - delta) * SCALE).astype(jnp.bfloat16)
            dv_acc[rows_of(t), :] += jnp.dot(pb, g_ref[...], preferred_element_type=jnp.float32)
            dk_acc[rows_of(t), :] += jnp.dot(ds, q_ref[...], preferred_element_type=jnp.float32)
            dqt_ref[...] += lax.dot_general(
                kv_ref[rows_of(t), :DH], ds, (((0,), (0,)), ((), ())),
                preferred_element_type=jnp.float32,
            )
            return 0

        lax.fori_loop(0, count, grads, 0)
        dq = dqt_ref[...].T.astype(jnp.bfloat16)
        for h in range(HEADS):
            dq_ref[s, :, h * DH:(h + 1) * DH] = dq[h * ROWS:(h + 1) * ROWS, :]
        return 0

    lax.fori_loop(0, SLOTS, one_slot, 0)

    def store(i, _):
        for core in range(2):
            for yh in range(2):
                for n in range(4):
                    sc, yl, sx, sz = place_of(core, yh, n, i)
                    place = order_ref[stored_block(yl, sc, yh, (x + sx) % 4, (z + sz) % 4)]
                    out = (mine if core == 0 else other)[yh * 4 + n]
                    out[block_rows(i), :DH] = dk_acc[block_rows(place), :].astype(out.dtype)
                    out[block_rows(i), DH:] = dv_acc[block_rows(place), :].astype(out.dtype)
        return 0

    lax.fori_loop(0, RUN, store, 0)


def attend(order, seg, qg, pieces):
    vmem = pl.BlockSpec(memory_space=pltpu.VMEM)
    piece = (PIECE, 2 * DH)
    result = pl.pallas_call(
        attend_kernel,
        out_shape=(
            jax.ShapeDtypeStruct((SLOTS, ROWS, HEADS * DH), jnp.bfloat16),
        )
        + (jax.ShapeDtypeStruct(piece, jnp.float32),) * 8
        + (jax.ShapeDtypeStruct(piece, jnp.bfloat16),) * 8,
        in_specs=[pl.BlockSpec(memory_space=pltpu.SMEM), vmem, vmem]
        + [pl.BlockSpec(memory_space=pltpu.HBM)] * 16,
        out_specs=(vmem,) * 17,
        scratch_shapes=[
            pltpu.VMEM((SEQ + TILE, 2 * DH), jnp.bfloat16),
            pltpu.VMEM((SEQ + TILE, DH), jnp.float32),
            pltpu.VMEM((SEQ + TILE, DH), jnp.float32),
            pltpu.VMEM((TILES * TILE, LANES), jnp.float32),
            pltpu.VMEM((DH, LANES), jnp.bfloat16),
            pltpu.VMEM((DH, LANES), jnp.bfloat16),
            pltpu.VMEM((LANES, DH), jnp.bfloat16),
            pltpu.VMEM((LANES, DH), jnp.bfloat16),
            pltpu.VMEM((DH, LANES), jnp.float32),
            pltpu.SemaphoreType.DMA,
        ],
        compiler_params=pltpu.CompilerParams(vmem_limit_bytes=48 * 1024 * 1024),
        cost_estimate=pl.CostEstimate(
            flops=8 * 10**9, bytes_accessed=12 * 10**6, transcendentals=8 * 10**6
        ),
        name="attend",
    )(order, seg, qg, *pieces)
    return result[0], result[1:9], result[9:]


def exchange(value, axes):
    return lax.all_to_all(value, axes, split_axis=0, concat_axis=0, tiled=True)


def ahead(value, axis, n):
    return lax.ppermute(value, axis, [(i, (i + n) % 4) for i in range(4)])


def other_core(value):
    return lax.ppermute(value, "c", [(0, 1), (1, 0)])


def added(terms):
    return sum(term.astype(jnp.float32) for term in terms)


def per_device(queries, keys, values, outputs, out_grads, block_order, segment_ids):
    kv = jnp.concatenate(
        [keys.reshape(ROWS, KVH, DH), values.reshape(ROWS, KVH, DH)], axis=-1
    ).transpose(1, 0, 2).reshape(KVH * ROWS, 2 * DH)
    kv = exchange(kv, Y)
    ways = (("z", "x"), ("x", "z"))
    halves = [kv[yh * 2 * ROWS:(yh + 1) * 2 * ROWS] for yh in range(2)]
    runs = [
        jnp.concatenate([half] + [ahead(half, way[0], n) for n in (1, 2, 3)], axis=0)
        for half, way in zip(halves, ways)
    ]
    runs = lax.optimization_barrier(runs)
    pieces = []
    for run, way in zip(runs, ways):
        pieces += [run] + [ahead(run, way[1], n) for n in (1, 2, 3)]
    pieces += [other_core(piece) for piece in pieces]

    products = outputs.astype(jnp.float32) * out_grads.astype(jnp.float32)
    delta = jnp.sum(products.reshape(ROWS, HQ, DH), axis=-1).T.reshape(SLOTS, 2, DH)
    high = lax.reduce_precision(delta, 8, 7)
    middle = lax.reduce_precision(delta - high, 8, 7)
    low = delta - high - middle
    parts = jnp.concatenate([high, middle, low], axis=1).astype(jnp.bfloat16)
    qg = jnp.concatenate(
        [
            queries.reshape(ROWS, SLOTS, HEADS * DH).transpose(1, 0, 2),
            out_grads.reshape(ROWS, SLOTS, HEADS * DH).transpose(1, 0, 2),
            jnp.pad(parts, ((0, 0), (0, ROWS - 6), (0, 0))),
        ],
        axis=-1,
    )
    qg = exchange(qg, YC)

    dq, mine, other = attend(block_order, segment_ids.reshape(SEQ // 128, 128), qg, pieces)

    back = (("x", "z"), ("z", "x"))
    both = [None] * 8
    for i in (1, 5, 3, 7, 2, 6, 0, 4):
        both[i] = (mine[i] + other_core(other[i]).astype(jnp.float32)).astype(jnp.bfloat16)
    parts = []
    for yh, way in enumerate(back):
        own, *sent = both[yh * 4:yh * 4 + 4]
        terms = [own] + [ahead(term, way[0], n) for n, term in zip((1, 2, 3), sent)]
        parts.append(added(terms).astype(jnp.bfloat16).reshape(4, 2 * ROWS, 2 * DH))
    parts = lax.optimization_barrier(parts)
    sums = []
    for part, way in zip(parts, back):
        terms = [part[0]] + [ahead(part[n], way[1], n) for n in (1, 2, 3)]
        sums.append(added(terms).astype(jnp.bfloat16))
    sums = exchange(jnp.concatenate(sums, axis=0), Y).reshape(KVH, ROWS, 2, DH)
    grad_keys = sums[:, :, 0].transpose(1, 0, 2).reshape(ROWS, KVH * DH)
    grad_values = sums[:, :, 1].transpose(1, 0, 2).reshape(ROWS, KVH * DH)
    grad_queries = exchange(dq, YC).transpose(1, 0, 2).reshape(ROWS, HQ * DH)
    return grad_queries, grad_keys, grad_values


def solution(mesh):
    split = Mesh(mesh.devices.reshape(SIZES), AXES)
    rows = P(AXES, None)
    return jax.shard_map(
        per_device,
        mesh=split,
        in_specs=(rows, rows, rows, rows, rows, P(), P()),
        out_specs=(rows, rows, rows),
        check_vma=False,
    )
```

```python
import math

import jax
import jax.numpy as jnp
from jax import lax
from jax.experimental import pallas as pl
from jax.experimental.pallas import tpu as pltpu
from jax.sharding import Mesh, PartitionSpec as P

HQ = 32
KVH = 4
DH = 128
ROWS = 64
SEQ = 8192
BLOCKS = 128
DOCS = 4
DOC_MOST = 4096
SLOTS = 8
HEADS = 4
LANES = HEADS * ROWS
TILE = 1024
TILES = (DOC_MOST + ROWS) // TILE + 2
RUN = 8
PIECE = RUN * ROWS

SCALE = 1.0 / math.sqrt(DH)
LOG2E = 1.0 / math.log(2.0)

AXES = ("yl", "c", "yh", "x", "z")
SIZES = (2, 2, 2, 4, 4)
YC = ("yh", "yl", "c")
Y = ("yh", "yl")


def stored_block(yl, c, yh, x, z):
    return (((yl * 2 + c) * 2 + yh) * 4 + x) * 4 + z


def block_rows(index):
    return pl.ds(pl.multiple_of(index * ROWS, ROWS), ROWS)


def attend_kernel(*refs):
    order_ref, seg_ref, qg_ref = refs[:3]
    pieces = refs[3:13]
    dq_ref, mine, other = refs[13], refs[14:16], refs[16:18]
    kv_ref, dk_acc, dv_acc, e_ref, qt_ref, gt_ref, q_ref, g_ref, dqt_ref = refs[18:]
    c, x, z = lax.axis_index("c"), lax.axis_index("x"), lax.axis_index("z")
    y = 2 * lax.axis_index("yh") + lax.axis_index("yl")

    def place_of(core, yh, far, i):
        near, yl = i // 2, i % 2
        sx, sz = (far, near) if yh == 0 else (near, far)
        sc = c if core == 0 else 1 - c
        return sc, yl, sx, sz

    def load(i, _):
        for core in range(2):
            for yh in range(2):
                for n in range(4):
                    sc, yl, sx, sz = place_of(core, yh, n, i)
                    sy = (y + 4 - 2 * yh - yl) % 4
                    place = order_ref[
                        stored_block(sy % 2, sc, sy // 2, (x + 4 - sx) % 4, (z + 4 - sz) % 4)
                    ]
                    source = pieces[yh * 4 + n] if core == 0 else pieces[8 + yh]
                    at = block_rows(i if core == 0 else n * RUN + i)
                    kv_ref[block_rows(place), :] = source[at, :]
        return 0

    lax.fori_loop(0, RUN, load, 0)

    kv_ref[SEQ:, :] = jnp.zeros((TILE, 2 * DH), jnp.bfloat16)
    dk_acc[...] = jnp.zeros_like(dk_acc)
    dv_acc[...] = jnp.zeros_like(dv_acc)
    seg = seg_ref[...]
    starts = [jnp.sum((seg < d).astype(jnp.int32)) for d in range(1, DOCS)]

    lane = lax.broadcasted_iota(jnp.int32, (1, LANES), 1)
    row_in_block = lane % ROWS
    tile_row = lax.broadcasted_iota(jnp.int32, (TILE, LANES), 0)

    def one_slot(s, _):
        place = order_ref[stored_block((s // 2) % 2, s % 2, s // 4, x, z)]
        first = place * ROWS
        lo = jnp.int32(0)
        lo_last = jnp.int32(0)
        row_pos = first + row_in_block
        row_lo = jnp.zeros((1, LANES), jnp.int32)
        for start in starts:
            lo = jnp.where(start <= first, start, lo)
            lo_last = jnp.where(start <= first + ROWS - 1, start, lo_last)
            row_lo = jnp.where(start <= row_pos, start, row_lo)
        base = lo // ROWS * ROWS
        length = first + ROWS - base
        count = (length + TILE // 2 - 1) // TILE
        ends = (length + TILE - 1) // TILE
        inner_lo = jnp.minimum((lo_last - base + TILE - 1) // TILE, count)
        inner_hi = jnp.maximum(jnp.minimum((first - base) // TILE, count), inner_lo)
        for h in range(HEADS):
            q_ref[h * ROWS:(h + 1) * ROWS, :] = qg_ref[s, :, h * DH:(h + 1) * DH]
            g_ref[h * ROWS:(h + 1) * ROWS, :] = qg_ref[s, :, (HEADS + h) * DH:(HEADS + h + 1) * DH]
        qt_ref[...] = q_ref[...].T
        gt_ref[...] = g_ref[...].T
        parts = qg_ref[s, :16, 2 * HEADS * DH:].astype(jnp.float32)
        delta = jnp.concatenate(
            [parts[i:i + 1] + parts[i + 2:i + 3] + parts[i + 4:i + 5] for i in range(2)], axis=1
        )

        def rows_of(t, size):
            return pl.ds(pl.multiple_of(base + t * TILE, ROWS), size)

        def kept(t, size):
            return pl.ds(pl.multiple_of(t * TILE, TILE), size)

        def scores(masked, size=TILE):
            def step(t, top):
                st = jnp.dot(
                    kv_ref[rows_of(t, size), :DH], qt_ref[...], preferred_element_type=jnp.float32
                )
                if masked:
                    pos = tile_row[:size] + (base + t * TILE)
                    st = jnp.where((pos <= row_pos) & (pos >= row_lo), st, -2e30)
                e_ref[kept(t, size), :] = st
                return jnp.maximum(top, jnp.max(st.reshape(size // 8, 8, LANES), axis=0))
            return step

        top = jnp.full((8, LANES), -1e30, jnp.float32)
        top = lax.fori_loop(0, inner_lo, scores(True), top)
        top = lax.fori_loop(inner_lo, inner_hi, scores(False), top)
        top = lax.fori_loop(inner_hi, count, scores(True), top)
        top = lax.fori_loop(count, ends, scores(True, TILE // 2), top)
        top = jnp.max(top, axis=0, keepdims=True) * (SCALE * LOG2E)

        def exps(size):
            def step(t, total):
                e = jnp.exp2(e_ref[kept(t, size), :] * (SCALE * LOG2E) - top)
                e_ref[kept(t, size), :] = e
                return total + jnp.sum(e.reshape(size // 8, 8, LANES), axis=0)
            return step

        total = lax.fori_loop(0, count, exps(TILE), jnp.zeros((8, LANES), jnp.float32))
        total = lax.fori_loop(count, ends, exps(TILE // 2), total)
        inverse = 1.0 / jnp.sum(total, axis=0, keepdims=True)
        dqt_ref[...] = jnp.zeros_like(dqt_ref)

        def grads(size):
            def step(t, _):
                p = e_ref[kept(t, size), :] * inverse
                dp = jnp.dot(kv_ref[rows_of(t, size), DH:], gt_ref[...], preferred_element_type=jnp.float32)
                pb = p.astype(jnp.bfloat16)
                ds = (p * (dp - delta) * SCALE).astype(jnp.bfloat16)
                dv_acc[rows_of(t, size), :] += jnp.dot(pb, g_ref[...], preferred_element_type=jnp.float32)
                dk_acc[rows_of(t, size), :] += jnp.dot(ds, q_ref[...], preferred_element_type=jnp.float32)
                dqt_ref[...] += lax.dot_general(
                    kv_ref[rows_of(t, size), :DH], ds, (((0,), (0,)), ((), ())),
                    preferred_element_type=jnp.float32,
                )
                return 0
            return step

        lax.fori_loop(0, count, grads(TILE), 0)
        lax.fori_loop(count, ends, grads(TILE // 2), 0)
        dq = dqt_ref[...].T.astype(jnp.bfloat16)
        for h in range(HEADS):
            dq_ref[s, :, h * DH:(h + 1) * DH] = dq[h * ROWS:(h + 1) * ROWS, :]
        return 0

    lax.fori_loop(0, SLOTS, one_slot, 0)

    def store(i, _):
        for core in range(2):
            for yh in range(2):
                for n in range(4):
                    sc, yl, sx, sz = place_of(core, yh, n, i)
                    place = order_ref[stored_block(yl, sc, yh, (x + sx) % 4, (z + sz) % 4)]
                    out = (mine if core == 0 else other)[yh]
                    dst = block_rows(n * RUN + i)
                    out[dst, :DH] = dk_acc[block_rows(place), :].astype(out.dtype)
                    out[dst, DH:] = dv_acc[block_rows(place), :].astype(out.dtype)
        return 0

    lax.fori_loop(0, RUN, store, 0)


def attend(order, seg, qg, pieces):
    vmem = pl.BlockSpec(memory_space=pltpu.VMEM)
    piece = (SEQ // 2 // 2, 2 * DH)
    result = pl.pallas_call(
        attend_kernel,
        out_shape=(
            jax.ShapeDtypeStruct((SLOTS, ROWS, HEADS * DH), jnp.bfloat16),
        )
        + (jax.ShapeDtypeStruct(piece, jnp.float32),) * 2
        + (jax.ShapeDtypeStruct(piece, jnp.bfloat16),) * 2,
        in_specs=[pl.BlockSpec(memory_space=pltpu.SMEM)] + [vmem] * 12,
        out_specs=(vmem,) * 5,
        scratch_shapes=[
            pltpu.VMEM((SEQ + TILE, 2 * DH), jnp.bfloat16),
            pltpu.VMEM((SEQ + TILE, DH), jnp.float32),
            pltpu.VMEM((SEQ + TILE, DH), jnp.float32),
            pltpu.VMEM((TILES * TILE, LANES), jnp.float32),
            pltpu.VMEM((DH, LANES), jnp.bfloat16),
            pltpu.VMEM((DH, LANES), jnp.bfloat16),
            pltpu.VMEM((LANES, DH), jnp.bfloat16),
            pltpu.VMEM((LANES, DH), jnp.bfloat16),
            pltpu.VMEM((DH, LANES), jnp.float32),
        ],
        compiler_params=pltpu.CompilerParams(vmem_limit_bytes=40 * 1024 * 1024),
        cost_estimate=pl.CostEstimate(
            flops=8 * 10**9, bytes_accessed=12 * 10**6, transcendentals=8 * 10**6
        ),
        name="attend",
    )(order, seg, qg, *pieces)
    return result[0], result[1:3], result[3:]


def exchange(value, axes):
    return lax.all_to_all(value, axes, split_axis=0, concat_axis=0, tiled=True)


def ahead(value, axis, n):
    return lax.ppermute(value, axis, [(i, (i + n) % 4) for i in range(4)])


def over_y(value, n):
    at = [place % 2 * 2 + place // 2 for place in range(4)]
    return lax.ppermute(value, ("yl", "yh"), [(at[i], at[(i + n) % 4]) for i in range(4)])


def other_core(value):
    return lax.ppermute(value, "c", [(0, 1), (1, 0)])


def added(terms):
    return sum(term.astype(jnp.float32) for term in terms)


def per_device(queries, keys, values, outputs, out_grads, block_order, segment_ids):
    kv = jnp.concatenate(
        [keys.reshape(ROWS, KVH, DH), values.reshape(ROWS, KVH, DH)], axis=-1
    ).transpose(1, 0, 2)
    y = lax.axis_index(Y)
    kv = [lax.dynamic_index_in_dim(kv, (y + n) % 4, 0, keepdims=False) for n in range(4)]
    kv = [kv[0]] + [over_y(kv[n], n) for n in (1, 2, 3)]
    ways = (("z", "x"), ("x", "z"))
    halves = [jnp.concatenate(kv[i:i + 2], axis=0) for i in (0, 2)]
    runs = [
        jnp.concatenate([half] + [ahead(half, way[0], n) for n in (1, 2, 3)], axis=0)
        for half, way in zip(halves, ways)
    ]
    products = outputs.astype(jnp.float32) * out_grads.astype(jnp.float32)
    delta = jnp.sum(products.reshape(ROWS, HQ, DH), axis=-1).T.reshape(SLOTS, 2, DH)
    high = lax.reduce_precision(delta, 8, 7)
    middle = lax.reduce_precision(delta - high, 8, 7)
    low = delta - high - middle
    parts = jnp.concatenate([high, middle, low], axis=1).astype(jnp.bfloat16)
    qg = jnp.concatenate(
        [
            queries.reshape(ROWS, SLOTS, HEADS * DH).transpose(1, 0, 2),
            out_grads.reshape(ROWS, SLOTS, HEADS * DH).transpose(1, 0, 2),
            jnp.pad(parts, ((0, 0), (0, ROWS - 6), (0, 0))),
        ],
        axis=-1,
    )
    runs = lax.optimization_barrier(runs)
    pieces = []
    for run, way in zip(runs, ways):
        pieces += [run] + [ahead(run, way[1], n) for n in (1, 2, 3)]

    qg = exchange(qg, YC)
    pieces, qg = lax.optimization_barrier((pieces, qg))
    pieces += [other_core(jnp.concatenate(pieces[i:i + 4], axis=0)) for i in (0, 4)]

    dq, mine, other = attend(block_order, segment_ids.reshape(SEQ // 128, 128), qg, pieces)

    back = (("x", "z"), ("z", "x"))
    came = [other_core(term) for term in other]
    both = []
    for own, term in zip(mine, came):
        half = (own + term.astype(jnp.float32)).astype(jnp.bfloat16)
        both += [half[i * PIECE:(i + 1) * PIECE] for i in range(4)]
    parts = []
    for yh, way in enumerate(back):
        own, *sent = both[yh * 4:yh * 4 + 4]
        terms = [own] + [ahead(term, way[0], n) for n, term in zip((1, 2, 3), sent)]
        parts.append(added(terms).astype(jnp.bfloat16).reshape(4, 2 * ROWS, 2 * DH))
    parts = lax.optimization_barrier(parts)
    sums = []
    for part, way in zip(parts, back):
        terms = [part[0]] + [ahead(part[n], way[1], n) for n in (1, 2, 3)]
        sums.append(added(terms).astype(jnp.bfloat16))
    sums = jnp.concatenate(sums, axis=0).reshape(KVH, ROWS, 2 * DH)
    sums = [lax.dynamic_index_in_dim(sums, (y + n) % 4, 0, keepdims=False) for n in range(4)]
    sums = jnp.stack([sums[0]] + [over_y(sums[n], n) for n in (1, 2, 3)])
    sums = [lax.dynamic_index_in_dim(sums, (y + 4 - g) % 4, 0, keepdims=False) for g in range(4)]
    sums = jnp.stack(sums).reshape(KVH, ROWS, 2, DH)
    grad_keys = sums[:, :, 0].transpose(1, 0, 2).reshape(ROWS, KVH * DH)
    grad_values = sums[:, :, 1].transpose(1, 0, 2).reshape(ROWS, KVH * DH)
    grad_queries = exchange(dq, YC).transpose(1, 0, 2).reshape(ROWS, HQ * DH)
    return grad_queries, grad_keys, grad_values


def solution(mesh):
    split = Mesh(mesh.devices.reshape(SIZES), AXES)
    rows = P(AXES, None)
    return jax.shard_map(
        per_device,
        mesh=split,
        in_specs=(rows, rows, rows, rows, rows, P(), P()),
        out_specs=(rows, rows, rows),
        check_vma=False,
    )
```
